256 devices in a mesh: blk: 16 (over x_hi, y, core), tm: 16 (over z, x_lo).
Axes of the slice: x: 4 (x_hi: 2, x_lo: 2; x = x_hi * 2 + x_lo), y: 4, z: 8, core: 2. Of those that a mesh axis runs over, the one named last changes fastest.
Arguments:
- occupied_orbitals: float32 [2048, 2048], P(None, 'blk'), may hold values from -0.6 to 0.6
- empty_orbitals: float32 [2048, 2048], P(None, 'blk'), may hold values from -0.6 to 0.6
- occupied_energy: float32 [2048], replicated, may hold values from -1.5 to -0.05
- empty_energy: float32 [2048], replicated, may hold values from 0.05 to 1.5
- time_points: float32 [16], replicated, may hold values from 0.25 to 4
- pair_table: int32 [16], replicated, may hold values from 0 to 15, each once
Outputs:
- polarizability: float32 [16, 2, 2048, 1024], P('tm', None, 'blk')
The draws below stay inside these ranges and needn't reach their ends.
Inputs may be any that keep to these rules, and one draw needn't show every extreme that they name: `pair_table`: each of 0 to 15 appears exactly once.
All inputs are finite; a program needn't handle non-finite values.
Results may differ from the reference program's by a relative error of at most 0.000088.
Values sent between devices are 32-bit elements; how exact they have to be, the bound alone decides.
A program may use at most 64 MiB of HBM per device.

```python
import math
import jax
import jax.numpy as jnp
from jax import lax

NST = 2048
TAU_DEV = 2
R = 2048
NPAIR = 16
N_TM = 16


def levels(stream_key, extent, cuts, smallest, top_value):
    level, own = 1.0, jax.random.fold_in(stream_key, 6)
    for axis_at, parts in cuts:
        draws = jnp.exp(jax.random.uniform(jax.random.fold_in(own, axis_at), (parts,), jnp.float32, smallest / len(cuts), top_value / len(cuts)))
        level = level * jnp.repeat(draws, extent[axis_at] // parts).reshape([-1 if axis == axis_at else 1 for axis in range(len(extent))])
    return level


def centred(stream_key, shape, spread, limit, pieces=(), kind=jnp.bfloat16):
    loudness = levels(stream_key, shape, pieces, -0.22, 0.18) if pieces else 1.0
    result = jax.random.normal(stream_key, shape, jnp.float32) * spread * loudness
    return jnp.minimum(jnp.maximum(result, -limit), limit).astype(kind)


def setup_inputs(seed: int = 0) -> dict:
    streams_of = jax.random.split(jax.random.key(seed), 7)
    occupied_orbitals = centred(streams_of[0], (NST, R), 0.1, 0.6, ((1, 16),), jnp.float32)
    empty_orbitals = centred(streams_of[1], (NST, R), 0.1, 0.6, ((1, 16),), jnp.float32)
    occupied_energy = jnp.clip(jax.random.uniform(streams_of[2], (NST,), jnp.float32, -1.5, -0.05), -1.5, -0.05)
    empty_energy = jnp.clip(jax.random.uniform(streams_of[3], (NST,), jnp.float32, 0.05, 1.5), 0.05, 1.5)
    time_points = jnp.clip(jnp.exp(jax.random.uniform(streams_of[4], (NPAIR,), jnp.float32, math.log(0.25), math.log(4.0))), 0.25, 4.0)
    pair_table = jax.random.permutation(streams_of[5], NPAIR).astype(jnp.int32)
    return dict(occupied_orbitals=occupied_orbitals, empty_orbitals=empty_orbitals, occupied_energy=occupied_energy, empty_energy=empty_energy, time_points=time_points, pair_table=pair_table)


def reference(occupied_orbitals, empty_orbitals, occupied_energy, empty_energy, time_points, pair_table):
    chosen = time_points[pair_table]

    def slot_field(moment):
        empty_weight = jnp.exp(-empty_energy * moment)
        occupied_weight = jnp.exp(occupied_energy * moment)
        empty_green = jnp.dot((empty_orbitals * empty_weight[:, None]).T, empty_orbitals,
                              precision=lax.Precision.HIGHEST, preferred_element_type=jnp.float32)
        occupied_green = jnp.dot((occupied_orbitals * occupied_weight[:, None]).T, occupied_orbitals,
                                 precision=lax.Precision.HIGHEST, preferred_element_type=jnp.float32)
        return -(empty_green * occupied_green)

    fields = lax.map(slot_field, chosen)
    fields = fields.reshape(N_TM // 2, TAU_DEV, R, 2, R // 2)
    fields = jnp.transpose(fields, (0, 3, 1, 2, 4))
    return fields.reshape(N_TM, TAU_DEV, R, R // 2)
```

```python
import jax
import jax.numpy as jnp
from jax import lax
from jax.experimental import pallas as pl
from jax.experimental.pallas import tpu as pltpu
from jax.sharding import PartitionSpec as P

MESH = pl.DeviceIdType.MESH
NZ = 8
NY = 4
F32 = jnp.float32
BF16 = jnp.bfloat16


def split(value):
    hi = value.astype(BF16)
    lo = (value - hi.astype(F32)).astype(BF16)
    return hi, lo


def kernel(occ_ref, emp_ref, occ_e_ref, emp_e_ref, time_ref, pair_ref, out_ref,
           turned, own, slices, rhs, lhs, weights, outgoing, arrived, result,
           ag_send, ag_recv, z_send, z_recv, mirror_send, mirror_recv, out_sem):
    states, width = occ_ref.shape
    piece = width // NZ
    blk, tm = lax.axis_index("blk"), lax.axis_index("tm")
    x_hi, y, c = lax.div(blk, 8), lax.rem(lax.div(blk, 2), NY), lax.rem(blk, 2)
    z, half = lax.div(tm, 2), lax.rem(tm, 2)
    home = x_hi == half
    column = lax.rem(blk, 8)

    def in_column(y_to, c_to):
        return (x_hi * 8 + lax.rem(y_to, NY) * 2 + c_to, tm)

    sibling = in_column(y, 1 - c)
    up, down = in_column(y + 1, c), in_column(y + 3, c)
    across = (half * 8 + y * 2 + c, z * 2 + x_hi)

    def z_peer(step):
        return (blk, lax.rem(z + step, NZ) * 2 + half)

    def block_of(q):
        group, flip = lax.div(q, 2), lax.rem(q, 2)
        dy = group ^ lax.div(group, 2)
        return half * 8 + lax.rem(y + dy, NY) * 2 + lax.rem(c + flip, 2)

    def mirror_of(q):
        return (block_of(q), z * 2 + x_hi)

    barrier = pltpu.get_barrier_semaphore()

    def greet(device):
        pl.semaphore_signal(barrier, inc=1, device_id=device, device_id_type=MESH)

    @pl.loop(1, NZ)
    def _(step):
        greet(z_peer(step))

    @pl.loop(1, 8)
    def _(q):
        greet(mirror_of(q))

    @pl.when(jnp.logical_not(home))
    def _():
        greet(across)
        greet(sibling)
        greet(up)
        greet(down)

    rows = lax.broadcasted_iota(jnp.int32, (16, 1), 0)
    moments = jnp.zeros((16, 1), F32)
    for row in range(16):
        moment = time_ref[pair_ref[2 * (row % 8) + row // 8]]
        moments = jnp.where(rows == row, moment, moments)
    weights[0] = jnp.exp(-emp_e_ref[...] * moments)
    weights[1] = jnp.exp(occ_e_ref[...] * moments)

    for kind, ref in enumerate((emp_ref, occ_ref)):
        @pl.loop(0, states // 256)
        def _(chunk):
            at = pl.ds(pl.multiple_of(chunk * 256, 256), 256)
            turned[kind, :, at] = ref[at, :].T
    own[...] = turned[:, pl.ds(pl.multiple_of(z * piece, piece), piece), :]

    @pl.when(home)
    def _():
        slices[0] = own[...]
        pl.semaphore_wait(barrier, 14)

    def gather_copy(source, at, device, n):
        return pltpu.make_async_remote_copy(
            src_ref=source, dst_ref=slices.at[at], send_sem=ag_send.at[n], recv_sem=ag_recv.at[at],
            device_id=device, device_id_type=MESH)

    cross = gather_copy(own, 0, across, 0)
    to_sibling = gather_copy(slices.at[0], 1, sibling, 1)
    to_up = gather_copy(slices.at[0], 4, up, 2)
    to_down = gather_copy(slices.at[0], 2, down, 3)

    @pl.when(jnp.logical_not(home))
    def _():
        pl.semaphore_wait(barrier, 18)
        cross.start()

    for kind, ref in enumerate((emp_ref, occ_ref)):
        @pl.loop(0, states // 256)
        def _(chunk):
            at = pl.ds(pl.multiple_of(chunk * 256, 256), 256)
            hi, lo = split(ref[at, :])
            rhs[kind, at, 0:width] = hi
            rhs[kind, at, width:] = lo

    @pl.when(jnp.logical_not(home))
    def _():
        cross.wait_recv()

    to_up.start()
    to_down.start()
    to_sibling.start()

    def z_copy(q, step):
        to = lax.rem(z + step, NZ)
        return pltpu.make_async_remote_copy(
            src_ref=outgoing.at[q, to], dst_ref=arrived.at[q, pl.ds(pl.multiple_of(z * piece, piece), piece)],
            send_sem=z_send.at[q], recv_sem=z_recv.at[q], device_id=z_peer(step), device_id_type=MESH)

    def compute(q, at, u):
        tiles = []
        for kind in range(2):
            values = slices[q, kind]
            for p in range(8):
                factor = weights[kind, pl.ds(pl.multiple_of(u * 8, 8), 8), :][p:p + 1, :]
                hi, lo = split(values * factor)
                lhs[kind, p * piece:(p + 1) * piece, :] = hi
                lhs[kind, 128 + p * piece:128 + (p + 1) * piece, :] = lo
            total = jnp.dot(lhs[kind], rhs[kind], preferred_element_type=F32)
            tiles.append((total[0:128, 0:width]
                          + (total[0:128, width:] + (total[128:, 0:width] + total[128:, width:]))))
        outgoing[at] = (-(tiles[0] * tiles[1])).reshape(8, piece, width)
        arrived[at, pl.ds(pl.multiple_of(z * piece, piece), piece), :] = outgoing[at, z]

        @pl.loop(1, NZ)
        def _(step):
            z_copy(at, step).start()

    def slot_of(q):
        return (block_of(q) < blk).astype(jnp.int32)

    def gathered(q):
        gather_copy(slices.at[q], q, sibling, 0).wait_recv()

    def receive(q):
        rest = arrived.at[q, pl.ds(0, (NZ - 1) * piece)]
        pltpu.make_async_copy(rest, rest, z_recv.at[q]).wait()

    def mirror_copy(q):
        return pltpu.make_async_remote_copy(
            src_ref=arrived.at[q], dst_ref=result.at[slot_of(q), :, pl.ds(pl.multiple_of(column * width, width), width)],
            send_sem=mirror_send.at[q], recv_sem=mirror_recv.at[column], device_id=mirror_of(q), device_id_type=MESH)

    def place(q, at, u):
        columns = pl.ds(pl.multiple_of(lax.rem(block_of(q), 8) * width, width), width)
        result[u, :, columns] = arrived[at].T

    def finish(q):
        receive(q)
        mirror_copy(q).start()
        place(q, q, slot_of(q))

    compute(0, 0, slot_of(0))

    @pl.when(home)
    def _():
        compute(0, 8, 1)

    gathered(1)
    compute(1, 1, slot_of(1))

    gathered(2)
    past_up = gather_copy(slices.at[2], 3, sibling, 4)
    past_up.start()
    gathered(4)
    past_down = gather_copy(slices.at[4], 5, sibling, 5)
    past_down.start()
    on_down = gather_copy(slices.at[2], 6, down, 6)
    on_up = gather_copy(slices.at[4], 6, up, 6)
    pl.when(c == 1)(on_down.start)
    pl.when(c == 0)(on_up.start)
    gathered(3)
    gathered(5)

    @pl.loop(2, 6)
    def _(q):
        compute(q, q, slot_of(q))

    gathered(6)
    far = gather_copy(slices.at[6], 7, sibling, 7)
    far.start()

    @pl.when(home)
    def _():
        receive(0)
        receive(8)
        place(0, 0, 0)
        place(0, 8, 1)

    @pl.when(jnp.logical_not(home))
    def _():
        finish(0)

    finish(1)
    compute(6, 6, slot_of(6))
    gathered(7)
    compute(7, 7, slot_of(7))

    @pl.loop(2, 8)
    def _(q):
        finish(q)

    def mirror_arrival(k):
        into = result.at[0, :, pl.ds(0, width)]
        pltpu.make_async_copy(into, into, mirror_recv.at[k]).wait()

    @pl.loop(0, 8)
    def _(k):
        @pl.when(jnp.logical_or(jnp.logical_not(home), k != column))
        def _():
            mirror_arrival(k)

    for u in range(2):
        pltpu.make_async_copy(result.at[u], out_ref.at[0, u], out_sem.at[u]).start()

    to_up.wait_send()
    to_down.wait_send()
    to_sibling.wait_send()
    past_up.wait_send()
    past_down.wait_send()
    on_up.wait_send()
    far.wait_send()

    def sent(q):
        rest = outgoing.at[q, pl.ds(0, NZ - 1)]
        pltpu.make_async_copy(rest, rest, z_send.at[q]).wait()

    @pl.loop(0, 8)
    def _(q):
        sent(q)

    @pl.loop(1, 8)
    def _(q):
        mirror_copy(q).wait_send()

    @pl.when(home)
    def _():
        sent(8)

    @pl.when(jnp.logical_not(home))
    def _():
        cross.wait_send()
        mirror_copy(0).wait_send()

    for u in range(2):
        pltpu.make_async_copy(result.at[u], out_ref.at[0, u], out_sem.at[u]).wait()


def body(occupied_orbitals, empty_orbitals, occupied_energy, empty_energy, time_points, pair_table):
    states, width = occupied_orbitals.shape
    piece = width // NZ
    vmem = pl.BlockSpec(memory_space=pltpu.VMEM)
    smem = pl.BlockSpec(memory_space=pltpu.SMEM)
    return pl.pallas_call(
        kernel,
        out_shape=jax.ShapeDtypeStruct((1, 2, width, 8 * width), F32),
        in_specs=[vmem, vmem, vmem, vmem, smem, smem],
        out_specs=pl.BlockSpec(memory_space=pl.ANY),
        scratch_shapes=[
            pltpu.VMEM((2, width, states), F32),
            pltpu.VMEM((2, piece, states), F32),
            pltpu.VMEM((8, 2, piece, states), F32),
            pltpu.VMEM((2, states, 2 * width), BF16),
            pltpu.VMEM((2, 256, states), BF16),
            pltpu.VMEM((2, 16, states), F32),
            pltpu.VMEM((9, NZ, piece, width), F32),
            pltpu.VMEM((9, width, width), F32),
            pltpu.VMEM((2, width, 8 * width), F32),
            pltpu.SemaphoreType.DMA((8,)),
            pltpu.SemaphoreType.DMA((8,)),
            pltpu.SemaphoreType.DMA((9,)),
            pltpu.SemaphoreType.DMA((9,)),
            pltpu.SemaphoreType.DMA((8,)),
            pltpu.SemaphoreType.DMA((8,)),
            pltpu.SemaphoreType.DMA((2,)),
        ],
        compiler_params=pltpu.CompilerParams(
            collective_id=0, has_side_effects=True, vmem_limit_bytes=40 * 2**20),
        cost_estimate=pl.CostEstimate(flops=2**33, bytes_accessed=2**22, transcendentals=2**16),
        name="polarizability",
    )(occupied_orbitals, empty_orbitals, occupied_energy.reshape(1, states), empty_energy.reshape(1, states),
      time_points, pair_table)


def solution(mesh):
    return jax.shard_map(
        body,
        mesh=mesh,
        in_specs=(P(None, "blk"), P(None, "blk"), P(), P(), P(), P()),
        out_specs=P("tm", None, "blk", None),
        check_vma=False,
    )
```

```python
import jax
import jax.numpy as jnp
from jax import lax
from jax.experimental import pallas as pl
from jax.experimental.pallas import tpu as pltpu
from jax.sharding import PartitionSpec as P

MESH = pl.DeviceIdType.MESH
NZ = 8
NY = 4
PARTS = 4
F32 = jnp.float32
BF16 = jnp.bfloat16


def split(value):
    hi = value.astype(BF16)
    lo = (value - hi.astype(F32)).astype(BF16)
    return hi, lo


def kernel(occ_hbm, emp_hbm, occ_e_hbm, emp_e_hbm, time_hbm, pair_hbm, out_ref,
           blocks, energies, time_ref, pair_ref, own, slices, rhs, lhs, weights, outgoing, arrived,
           load_sem, small_sem, ag_send, ag_recv, z_send, z_recv, mirror_send, mirror_recv):
    states, width = blocks.shape[1:]
    piece = width // NZ
    depth = states // PARTS
    blk, tm = lax.axis_index("blk"), lax.axis_index("tm")
    x_hi, y, c = lax.div(blk, 8), lax.rem(lax.div(blk, 2), NY), lax.rem(blk, 2)
    z, half = lax.div(tm, 2), lax.rem(tm, 2)
    home = x_hi == half
    away = jnp.logical_not(home)
    column = lax.rem(blk, 8)

    def in_column(y_to, c_to):
        return (x_hi * 8 + lax.rem(y_to, NY) * 2 + c_to, tm)

    sibling = in_column(y, 1 - c)
    up, down = in_column(y + 1, c), in_column(y + 3, c)
    across = (half * 8 + y * 2 + c, z * 2 + x_hi)

    def z_peer(step):
        return (blk, lax.rem(z + step, NZ) * 2 + half)

    def block_of(q):
        group, flip = lax.div(q, 2), lax.rem(q, 2)
        dy = group ^ lax.div(group, 2)
        return half * 8 + lax.rem(y + dy, NY) * 2 + lax.rem(c + flip, 2)

    def mirror_of(q):
        return (block_of(q), z * 2 + x_hi)

    loads = []
    for part in range(PARTS):
        rows = pl.ds(part * depth, depth)
        loads.append([pltpu.make_async_copy(ref.at[rows], blocks.at[kind, rows], load_sem.at[part, kind])
                      for kind, ref in enumerate((emp_hbm, occ_hbm))])
    small = [pltpu.make_async_copy(source, to, small_sem.at[n]) for n, (source, to) in enumerate((
        (emp_e_hbm, energies.at[0]), (occ_e_hbm, energies.at[1]), (time_hbm, time_ref), (pair_hbm, pair_ref)))]
    for pair in loads:
        for copy in pair:
            copy.start()
    for copy in small:
        copy.start()

    barrier = pltpu.get_barrier_semaphore()

    def greet(device):
        pl.semaphore_signal(barrier, inc=1, device_id=device, device_id_type=MESH)

    @pl.loop(1, NZ)
    def _(step):
        greet(z_peer(step))

    @pl.loop(1, 8)
    def _(q):
        greet(mirror_of(q))

    @pl.when(away)
    def _():
        greet(across)
        greet(sibling)
        greet(up)
        greet(down)

    def gather_copy(source, at, part, device, n):
        return pltpu.make_async_remote_copy(
            src_ref=source.at[part], dst_ref=slices.at[at, part], send_sem=ag_send.at[n],
            recv_sem=ag_recv.at[at, part if at % 2 == 0 else 0], device_id=device, device_id_type=MESH)

    def cross(part):
        return gather_copy(own, 0, part, across, 0)

    def spread(part):
        for at, device, n in ((4, up, 1), (2, down, 2), (1, sibling, 3)):
            gather_copy(slices.at[0], at, part, device, n).start()

    for part in range(PARTS):
        for kind in range(2):
            loads[part][kind].wait()
            turned = pltpu.roll(blocks[kind, part * depth:(part + 1) * depth, :],
                                lax.rem((NZ - z) * piece, width), 1).T[0:piece]

            @pl.when(home)
            def _():
                slices[0, part, kind] = turned

            @pl.when(away)
            def _():
                own[part, kind] = turned

        @pl.when(home)
        def _():
            if part == 0:
                pl.semaphore_wait(barrier, 14)
            spread(part)

        @pl.when(away)
        def _():
            if part == 0:
                pl.semaphore_wait(barrier, 18)
            cross(part).start()

    for copy in small:
        copy.wait()
    rows = lax.broadcasted_iota(jnp.int32, (16, 1), 0)
    moments = jnp.zeros((16, 1), F32)
    for row in range(16):
        moment = time_ref[pair_ref[2 * (row % 8) + row // 8]]
        moments = jnp.where(rows == row, moment, moments)
    weights[0] = jnp.exp(-energies[0] * moments)
    weights[1] = jnp.exp(energies[1] * moments)

    for part in range(PARTS):
        for kind in range(2):
            hi, lo = split(blocks[kind, part * depth:(part + 1) * depth, :])
            rhs[kind, part * depth:(part + 1) * depth, 0:width] = hi
            rhs[kind, part * depth:(part + 1) * depth, width:] = lo

        @pl.when(away)
        def _():
            cross(part).wait_recv()
            spread(part)

    def slot_of(q):
        return (block_of(q) < blk).astype(jnp.int32)

    def compute(work):
        rows = 128 * len(work)
        tiles = []
        for kind in range(2):
            for n, (q, at, u) in enumerate(work):
                for part in range(PARTS):
                    columns = slice(part * depth, (part + 1) * depth)
                    values = slices[q, part, kind]
                    factors = weights[kind, pl.ds(pl.multiple_of(u * 8, 8), 8), columns]
                    for p in range(8):
                        hi, lo = split(values * factors[p:p + 1, :])
                        lhs[kind, n * 128 + p * piece:n * 128 + (p + 1) * piece, columns] = hi
                        lhs[kind, rows + n * 128 + p * piece:rows + n * 128 + (p + 1) * piece, columns] = lo
            total = jnp.dot(lhs[kind, 0:2 * rows], rhs[kind], preferred_element_type=F32)
            tiles.append((total[0:rows, 0:width]
                          + (total[0:rows, width:] + (total[rows:, 0:width] + total[rows:, width:]))))
        product = -(tiles[0] * tiles[1])
        for n, (q, at, u) in enumerate(work):
            outgoing[at] = product[n * 128:(n + 1) * 128].reshape(NZ, piece, width)
            arrived[at, pl.ds(pl.multiple_of(z * piece, piece), piece), :] = outgoing[at, z]

    def z_copy(first, count, group, step):
        to = lax.rem(z + step, NZ)
        these = pl.ds(first, count)
        return pltpu.make_async_remote_copy(
            src_ref=outgoing.at[these, to],
            dst_ref=arrived.at[these, pl.ds(pl.multiple_of(z * piece, piece), piece)],
            send_sem=z_send.at[group], recv_sem=z_recv.at[group], device_id=z_peer(step), device_id_type=MESH)

    def share(first, count, group):
        @pl.loop(1, NZ)
        def _(step):
            z_copy(first, count, group, step).start()

    def pair(group):
        first = 2 * group
        compute([(first, first, slot_of(first)), (first + 1, first + 1, slot_of(first + 1))])
        share(first, 2, group)

    def gathered(q):
        whole = slices.at[q]
        pltpu.make_async_copy(whole, whole, ag_recv.at[q, 0]).wait()

    def relay(part):
        gather_copy(slices.at[0], 2, part, down, 2).wait_recv()
        gather_copy(slices.at[2], 3, part, sibling, 4).start()
        gather_copy(slices.at[0], 4, part, up, 1).wait_recv()
        gather_copy(slices.at[4], 5, part, sibling, 5).start()

        @pl.when(c == 1)
        def _():
            gather_copy(slices.at[2], 6, part, down, 6).start()

        @pl.when(c == 0)
        def _():
            gather_copy(slices.at[4], 6, part, up, 6).start()

    def relay_far(part):
        gather_copy(slices.at[4], 6, part, up, 6).wait_recv()
        gather_copy(slices.at[6], 7, part, sibling, 7).start()

    def receive(first, count, group):
        rest = arrived.at[pl.ds(first, count), pl.ds(0, (NZ - 1) * piece)]
        pltpu.make_async_copy(rest, rest, z_recv.at[group]).wait()

    def columns_of(k):
        return pl.ds(pl.multiple_of(k * width, width), width)

    def mirror_copy(q):
        return pltpu.make_async_remote_copy(
            src_ref=arrived.at[q], dst_ref=out_ref.at[0, slot_of(q), :, columns_of(column)],
            send_sem=mirror_send.at[q], recv_sem=mirror_recv.at[column], device_id=mirror_of(q), device_id_type=MESH)

    def place(q, at, u):
        out_ref[0, u, :, columns_of(lax.rem(block_of(q), 8))] = arrived[at].T

    def finish(group):
        first = 2 * group
        receive(first, 2, group)
        mirror_copy(first).start()
        mirror_copy(first + 1).start()
        place(first, first, slot_of(first))
        place(first + 1, first + 1, slot_of(first + 1))

    @pl.when(home)
    def _():
        compute([(0, 8, 1)])
        share(8, 1, 4)

    relay(0)
    relay(1)
    gathered(1)
    pair(0)
    relay(2)
    relay(3)
    gathered(3)
    pair(1)
    relay_far(0)
    relay_far(1)
    gathered(5)
    pair(2)
    relay_far(2)
    relay_far(3)

    @pl.when(home)
    def _():
        receive(8, 1, 4)
        place(0, 8, 1)
        receive(0, 2, 0)
        mirror_copy(1).start()
        place(0, 0, 0)
        place(1, 1, slot_of(1))

    @pl.when(away)
    def _():
        finish(0)

    gathered(7)
    pair(3)

    @pl.loop(1, 4)
    def _(group):
        finish(group)

    @pl.loop(0, 8)
    def _(k):
        @pl.when(jnp.logical_or(away, k != column))
        def _():
            into = out_ref.at[0, 0, :, columns_of(0)]
            pltpu.make_async_copy(into, into, mirror_recv.at[k]).wait()

    def sent(first, count, group):
        rest = outgoing.at[pl.ds(first, count), pl.ds(0, NZ - 1)]
        pltpu.make_async_copy(rest, rest, z_send.at[group]).wait()

    for n in range(1, 8):
        whole = slices.at[0]
        pltpu.make_async_copy(whole, whole, ag_send.at[n]).wait()

    @pl.loop(0, 4)
    def _(group):
        sent(2 * group, 2, group)

    @pl.loop(1, 8)
    def _(q):
        mirror_copy(q).wait_send()

    @pl.when(home)
    def _():
        sent(8, 1, 4)

    @pl.when(away)
    def _():
        pltpu.make_async_copy(own, own, ag_send.at[0]).wait()
        mirror_copy(0).wait_send()


def body(occupied_orbitals, empty_orbitals, occupied_energy, empty_energy, time_points, pair_table):
    states, width = occupied_orbitals.shape
    piece = width // NZ
    depth = states // PARTS
    return pl.pallas_call(
        kernel,
        out_shape=pltpu.VMEM((1, 2, width, 8 * width), F32),
        in_specs=[pl.BlockSpec(memory_space=pltpu.HBM)] * 6,
        out_specs=pl.BlockSpec(memory_space=pltpu.VMEM),
        scratch_shapes=[
            pltpu.VMEM((2, states, width), F32),
            pltpu.VMEM((2, 1, states), F32),
            pltpu.SMEM((16,), F32),
            pltpu.SMEM((16,), jnp.int32),
            pltpu.VMEM((PARTS, 2, piece, depth), F32),
            pltpu.VMEM((8, PARTS, 2, piece, depth), F32),
            pltpu.VMEM((2, states, 2 * width), BF16),
            pltpu.VMEM((2, 512, states), BF16),
            pltpu.VMEM((2, 16, states), F32),
            pltpu.VMEM((9, NZ, piece, width), F32),
            pltpu.VMEM((9, width, width), F32),
            pltpu.SemaphoreType.DMA((PARTS, 2)),
            pltpu.SemaphoreType.DMA((4,)),
            pltpu.SemaphoreType.DMA((8,)),
            pltpu.SemaphoreType.DMA((8, PARTS)),
            pltpu.SemaphoreType.DMA((5,)),
            pltpu.SemaphoreType.DMA((5,)),
            pltpu.SemaphoreType.DMA((8,)),
            pltpu.SemaphoreType.DMA((8,)),
        ],
        compiler_params=pltpu.CompilerParams(
            collective_id=0, has_side_effects=True, vmem_limit_bytes=61 * 2**20),
        cost_estimate=pl.CostEstimate(flops=2**33, bytes_accessed=2**22, transcendentals=2**16),
        name="polarizability",
    )(occupied_orbitals, empty_orbitals, occupied_energy.reshape(1, states), empty_energy.reshape(1, states),
      time_points, pair_table)


def solution(mesh):
    return jax.shard_map(
        body,
        mesh=mesh,
        in_specs=(P(None, "blk"), P(None, "blk"), P(), P(), P(), P()),
        out_specs=P("tm", None, "blk", None),
        check_vma=False,
    )
```

```python
import jax
import jax.numpy as jnp
from jax import lax
from jax.experimental import pallas as pl
from jax.experimental.pallas import tpu as pltpu
from jax.sharding import PartitionSpec as P

MESH = pl.DeviceIdType.MESH
NZ = 8
NY = 4
PARTS = 8
F32 = jnp.float32
BF16 = jnp.bfloat16


def split(value):
    hi = value.astype(BF16)
    lo = (value - hi.astype(F32)).astype(BF16)
    return hi, lo


def kernel(occ_hbm, emp_hbm, occ_e_hbm, emp_e_hbm, time_hbm, pair_hbm, out_ref,
           blocks, energies, time_ref, pair_ref, own, slices, rhs, lhs, weights, outgoing, arrived,
           load_sem, small_sem, ag_send, ag_recv, z_send, z_recv, mirror_send, mirror_recv):
    states, width = blocks.shape[1:]
    piece = width // NZ
    depth = states // PARTS
    blk, tm = lax.axis_index("blk"), lax.axis_index("tm")
    x_hi, y, c = lax.div(blk, 8), lax.rem(lax.div(blk, 2), NY), lax.rem(blk, 2)
    z, half = lax.div(tm, 2), lax.rem(tm, 2)
    home = x_hi == half
    away = jnp.logical_not(home)
    column = lax.rem(blk, 8)

    def in_column(y_to, c_to):
        return (x_hi * 8 + lax.rem(y_to, NY) * 2 + c_to, tm)

    sibling = in_column(y, 1 - c)
    up, down = in_column(y + 1, c), in_column(y + 3, c)
    across = (half * 8 + y * 2 + c, z * 2 + x_hi)

    def z_peer(step):
        return (blk, lax.rem(z + step, NZ) * 2 + half)

    def block_of(q):
        group, flip = lax.div(q, 2), lax.rem(q, 2)
        dy = group ^ lax.div(group, 2)
        return half * 8 + lax.rem(y + dy, NY) * 2 + lax.rem(c + flip, 2)

    def mirror_of(q):
        return (block_of(q), z * 2 + x_hi)

    loads = []
    for part in range(PARTS):
        rows = pl.ds(part * depth, depth)
        loads.append([pltpu.make_async_copy(ref.at[rows], blocks.at[kind, rows], load_sem.at[part, kind])
                      for kind, ref in enumerate((emp_hbm, occ_hbm))])
    small = [pltpu.make_async_copy(source, to, small_sem.at[n]) for n, (source, to) in enumerate((
        (emp_e_hbm, energies.at[0]), (occ_e_hbm, energies.at[1]), (time_hbm, time_ref), (pair_hbm, pair_ref)))]
    for pair in loads[:2]:
        for copy in pair:
            copy.start()
    for copy in small:
        copy.start()

    barrier = pltpu.get_barrier_semaphore()

    def greet(device):
        pl.semaphore_signal(barrier, inc=1, device_id=device, device_id_type=MESH)

    @pl.loop(1, NZ)
    def _(step):
        greet(z_peer(step))

    @pl.loop(1, 8)
    def _(q):
        greet(mirror_of(q))

    @pl.when(away)
    def _():
        greet(across)
        greet(sibling)
        greet(up)
        greet(down)

    def gather_copy(source, at, part, device, n):
        return pltpu.make_async_remote_copy(
            src_ref=source.at[part], dst_ref=slices.at[at, part], send_sem=ag_send.at[n],
            recv_sem=ag_recv.at[at, part if at % 2 == 0 else 0], device_id=device, device_id_type=MESH)

    def cross(part):
        return gather_copy(own, 0, part, across, 0)

    def spread(part):
        for at, device, n in ((4, up, 1), (2, down, 2), (1, sibling, 3)):
            gather_copy(slices.at[0], at, part, device, n).start()

    for part in range(PARTS):
        for kind in range(2):
            loads[part][kind].wait()
            if part + 2 < PARTS:
                loads[part + 2][kind].start()
            turned = pltpu.roll(blocks[kind, part * depth:(part + 1) * depth, :],
                                lax.rem((NZ - z) * piece, width), 1).T[0:piece]

            @pl.when(home)
            def _():
                slices[0, part, kind] = turned

            @pl.when(away)
            def _():
                own[part, kind] = turned

        @pl.when(home)
        def _():
            if part == 0:
                pl.semaphore_wait(barrier, 14)
            spread(part)

        @pl.when(away)
        def _():
            if part == 0:
                pl.semaphore_wait(barrier, 18)
            cross(part).start()

    for copy in small:
        copy.wait()
    rows = lax.broadcasted_iota(jnp.int32, (16, 1), 0)
    moments = jnp.zeros((16, 1), F32)
    for row in range(16):
        moment = time_ref[pair_ref[2 * (row % 8) + row // 8]]
        moments = jnp.where(rows == row, moment, moments)
    weights[0] = jnp.exp(-energies[0] * moments)
    weights[1] = jnp.exp(energies[1] * moments)

    for part in range(PARTS):
        for kind in range(2):
            hi, lo = split(blocks[kind, part * depth:(part + 1) * depth, :])
            rhs[kind, part * depth:(part + 1) * depth, 0:width] = hi
            rhs[kind, part * depth:(part + 1) * depth, width:] = lo

        @pl.when(away)
        def _():
            cross(part).wait_recv()
            spread(part)

    def slot_of(q):
        return (block_of(q) < blk).astype(jnp.int32)

    def compute(work):
        rows = 128 * len(work)
        tiles = []
        for kind in range(2):
            for n, (q, at, u) in enumerate(work):
                for part in range(PARTS):
                    columns = slice(part * depth, (part + 1) * depth)
                    values = slices[q, part, kind]
                    factors = weights[kind, pl.ds(pl.multiple_of(u * 8, 8), 8), columns]
                    for p in range(8):
                        hi, lo = split(values * factors[p:p + 1, :])
                        lhs[kind, n * 128 + p * piece:n * 128 + (p + 1) * piece, columns] = hi
                        lhs[kind, rows + n * 128 + p * piece:rows + n * 128 + (p + 1) * piece, columns] = lo
            total = jnp.dot(lhs[kind, 0:2 * rows], rhs[kind], preferred_element_type=F32)
            tiles.append((total[0:rows, 0:width]
                          + (total[0:rows, width:] + (total[rows:, 0:width] + total[rows:, width:]))))
        product = -(tiles[0] * tiles[1])
        for n, (q, at, u) in enumerate(work):
            outgoing[at] = product[n * 128:(n + 1) * 128].reshape(NZ, piece, width)
            arrived[at, pl.ds(pl.multiple_of(z * piece, piece), piece), :] = outgoing[at, z]

    def rows_of(plane):
        return pl.ds(pl.multiple_of(plane * piece, piece), piece)

    def far_first(n):
        return 4 + lax.div(n + 1, 2) * (1 - 2 * lax.rem(n, 2))

    def z_copy(first, count, group, step):
        to = lax.rem(z + step, NZ)
        these = pl.ds(first, count)
        return pltpu.make_async_remote_copy(
            src_ref=outgoing.at[these, to], dst_ref=arrived.at[these, rows_of(z)],
            send_sem=z_send.at[group], recv_sem=z_recv.at[group, step], device_id=z_peer(step), device_id_type=MESH)

    def share(first, count, group):
        @pl.loop(0, NZ - 1)
        def _(n):
            z_copy(first, count, group, far_first(n)).start()

    def columns_of(k):
        return pl.ds(pl.multiple_of(k * width, width), width)

    def mirror_copy(q, plane):
        return pltpu.make_async_remote_copy(
            src_ref=arrived.at[q, rows_of(plane)], dst_ref=out_ref.at[0, slot_of(q), rows_of(plane), columns_of(column)],
            send_sem=mirror_send.at[q], recv_sem=mirror_recv.at[column], device_id=mirror_of(q), device_id_type=MESH)

    def pair(group):
        first = 2 * group
        compute([(first, first, slot_of(first)), (first + 1, first + 1, slot_of(first + 1))])
        share(first, 2, group)

        @pl.when(jnp.logical_or(away, group > 0))
        def _():
            mirror_copy(first, z).start()

        mirror_copy(first + 1, z).start()

    def gathered(q):
        whole = slices.at[q]
        pltpu.make_async_copy(whole, whole, ag_recv.at[q, 0]).wait()

    def relay(part):
        gather_copy(slices.at[0], 2, part, down, 2).wait_recv()
        gather_copy(slices.at[2], 3, part, sibling, 4).start()
        gather_copy(slices.at[0], 4, part, up, 1).wait_recv()
        gather_copy(slices.at[4], 5, part, sibling, 5).start()

        @pl.when(c == 1)
        def _():
            gather_copy(slices.at[2], 6, part, down, 6).start()

        @pl.when(c == 0)
        def _():
            gather_copy(slices.at[4], 6, part, up, 6).start()

    def relay_far(part):
        gather_copy(slices.at[4], 6, part, up, 6).wait_recv()
        gather_copy(slices.at[6], 7, part, sibling, 7).start()

    def receive(first, count, group):
        @pl.loop(0, NZ - 1)
        def _(n):
            step = far_first(n)
            plane = lax.rem(z + NZ - step, NZ)
            here = arrived.at[pl.ds(first, count), rows_of(plane)]
            pltpu.make_async_copy(here, here, z_recv.at[group, step]).wait()
            if count == 2:
                @pl.when(jnp.logical_or(away, group > 0))
                def _():
                    mirror_copy(first, plane).start()

                mirror_copy(first + 1, plane).start()

    def place(q, at, u):
        out_ref[0, u, :, columns_of(lax.rem(block_of(q), 8))] = arrived[at].T

    def finish(group):
        first = 2 * group
        receive(first, 2, group)
        place(first, first, slot_of(first))
        place(first + 1, first + 1, slot_of(first + 1))

    @pl.when(home)
    def _():
        compute([(0, 8, 1)])
        share(8, 1, 4)

    def each(action, parts):
        for part in parts:
            action(part)

    early, late = range(PARTS // 2), range(PARTS // 2, PARTS)
    each(relay, early)
    gathered(1)
    pair(0)
    each(relay, late)
    gathered(3)
    pair(1)
    each(relay_far, early)
    gathered(5)
    pair(2)
    each(relay_far, late)

    @pl.when(home)
    def _():
        receive(8, 1, 4)
        place(0, 8, 1)

    finish(0)
    gathered(7)
    pair(3)

    @pl.loop(1, 4)
    def _(group):
        finish(group)

    @pl.loop(0, 8)
    def _(k):
        @pl.when(jnp.logical_or(away, k != column))
        def _():
            into = out_ref.at[0, 0, :, columns_of(0)]
            pltpu.make_async_copy(into, into, mirror_recv.at[k]).wait()

    def sent(first, count, group):
        rest = outgoing.at[pl.ds(first, count), pl.ds(0, NZ - 1)]
        pltpu.make_async_copy(rest, rest, z_send.at[group]).wait()

    for n in range(1, 8):
        whole = slices.at[0]
        pltpu.make_async_copy(whole, whole, ag_send.at[n]).wait()

    @pl.loop(0, 4)
    def _(group):
        sent(2 * group, 2, group)

    def mirrored(q):
        whole = arrived.at[q]
        pltpu.make_async_copy(whole, whole, mirror_send.at[q]).wait()

    @pl.loop(1, 8)
    def _(q):
        mirrored(q)

    @pl.when(home)
    def _():
        sent(8, 1, 4)

    @pl.when(away)
    def _():
        pltpu.make_async_copy(own, own, ag_send.at[0]).wait()
        mirrored(0)


def body(occupied_orbitals, empty_orbitals, occupied_energy, empty_energy, time_points, pair_table):
    states, width = occupied_orbitals.shape
    piece = width // NZ
    depth = states // PARTS
    return pl.pallas_call(
        kernel,
        out_shape=pltpu.VMEM((1, 2, width, 8 * width), F32),
        in_specs=[pl.BlockSpec(memory_space=pltpu.HBM)] * 6,
        out_specs=pl.BlockSpec(memory_space=pltpu.VMEM),
        scratch_shapes=[
            pltpu.VMEM((2, states, width), F32),
            pltpu.VMEM((2, 1, states), F32),
            pltpu.SMEM((16,), F32),
            pltpu.SMEM((16,), jnp.int32),
            pltpu.VMEM((PARTS, 2, piece, depth), F32),
            pltpu.VMEM((8, PARTS, 2, piece, depth), F32),
            pltpu.VMEM((2, states, 2 * width), BF16),
            pltpu.VMEM((2, 512, states), BF16),
            pltpu.VMEM((2, 16, states), F32),
            pltpu.VMEM((9, NZ, piece, width), F32),
            pltpu.VMEM((9, width, width), F32),
            pltpu.SemaphoreType.DMA((PARTS, 2)),
            pltpu.SemaphoreType.DMA((4,)),
            pltpu.SemaphoreType.DMA((8,)),
            pltpu.SemaphoreType.DMA((8, PARTS)),
            pltpu.SemaphoreType.DMA((5,)),
            pltpu.SemaphoreType.DMA((5, NZ)),
            pltpu.SemaphoreType.DMA((8,)),
            pltpu.SemaphoreType.DMA((8,)),
        ],
        compiler_params=pltpu.CompilerParams(
            collective_id=0, has_side_effects=True, vmem_limit_bytes=61 * 2**20),
        cost_estimate=pl.CostEstimate(flops=2**33, bytes_accessed=2**22, transcendentals=2**16),
        name="polarizability",
    )(occupied_orbitals, empty_orbitals, occupied_energy.reshape(1, states), empty_energy.reshape(1, states),
      time_points, pair_table)


def solution(mesh):
    return jax.shard_map(
        body,
        mesh=mesh,
        in_specs=(P(None, "blk"), P(None, "blk"), P(), P(), P(), P()),
        out_specs=P("tm", None, "blk", None),
        check_vma=False,
    )
```

```python
import jax
import jax.numpy as jnp
from jax import lax
from jax.experimental import pallas as pl
from jax.experimental.pallas import tpu as pltpu
from jax.sharding import PartitionSpec as P

MESH = pl.DeviceIdType.MESH
NZ = 8
NY = 4
PARTS = 8
LOADS = 4
SLOTS = ((0, 0), (0, 1), (1, 0), (3, 0), (1, 1), (3, 1), (2, 0), (2, 1))
DIRECT = (0, 2, 3, 6)
DOUBLE = (7, 6)
F32 = jnp.float32
BF16 = jnp.bfloat16


def split(value):
    hi = value.astype(BF16)
    lo = (value - hi.astype(F32)).astype(BF16)
    return hi, lo


def kernel(occ_hbm, emp_hbm, occ_e_hbm, emp_e_hbm, time_hbm, pair_hbm, out_ref,
           blocks, energies, time_ref, pair_ref, slices, rhs, lhs, weights, outgoing, arrived,
           load_sem, small_sem, ag_send, ag_recv, z_send, z_recv, mirror_send, mirror_recv):
    states, width = blocks.shape[1:]
    piece = width // NZ
    depth = states // PARTS
    own = slices.at[8]
    blk, tm = lax.axis_index("blk"), lax.axis_index("tm")
    x_hi, y, c = lax.div(blk, 8), lax.rem(lax.div(blk, 2), NY), lax.rem(blk, 2)
    z, half = lax.div(tm, 2), lax.rem(tm, 2)
    home = x_hi == half
    away = jnp.logical_not(home)
    column = lax.rem(blk, 8)

    def in_column(y_to, c_to):
        return (x_hi * 8 + lax.rem(y_to, NY) * 2 + c_to, tm)

    sibling = in_column(y, 1 - c)
    up, down = in_column(y + 1, c), in_column(y + 3, c)
    across = (half * 8 + y * 2 + c, z * 2 + x_hi)

    def z_peer(step):
        return (blk, lax.rem(z + step, NZ) * 2 + half)

    def block_of(q):
        dy, flip = SLOTS[q]
        return half * 8 + lax.rem(y + dy, NY) * 2 + lax.rem(c + flip, 2)

    def mirror_of(q):
        return (block_of(q), z * 2 + x_hi)

    loads = []
    for n in range(LOADS):
        rows = pl.ds(n * (states // LOADS), states // LOADS)
        loads.append([pltpu.make_async_copy(ref.at[rows], blocks.at[kind, rows], load_sem.at[n, kind])
                      for kind, ref in enumerate((emp_hbm, occ_hbm))])
    small = [pltpu.make_async_copy(source, to, small_sem.at[n]) for n, (source, to) in enumerate((
        (emp_e_hbm, energies.at[0]), (occ_e_hbm, energies.at[1]), (time_hbm, time_ref), (pair_hbm, pair_ref)))]
    for copy in loads[0]:
        copy.start()

    barrier = pltpu.get_barrier_semaphore()

    def greet(device):
        pl.semaphore_signal(barrier, inc=1, device_id=device, device_id_type=MESH)

    @pl.loop(1, NZ)
    def _(step):
        greet(z_peer(step))

    for q in range(1, 8):
        if q not in DOUBLE:
            greet(mirror_of(q))

    @pl.when(away)
    def _():
        greet(across)
        greet(sibling)
        greet(up)
        greet(down)

    for pair in loads[1:]:
        for copy in pair:
            copy.start()
    for copy in small:
        copy.start()

    def gather_copy(source, at, part, device, n):
        return pltpu.make_async_remote_copy(
            src_ref=source.at[part], dst_ref=slices.at[at, part], send_sem=ag_send.at[n],
            recv_sem=ag_recv.at[at, part if at in DIRECT else 0], device_id=device, device_id_type=MESH)

    def cross(part):
        return gather_copy(own, 0, part, across, 0)

    def spread(part):
        for at, device, n in ((3, up, 1), (2, down, 2), (1, sibling, 3)):
            gather_copy(slices.at[0], at, part, device, n).start()

    mine = jnp.where(home, 0, 8)
    run = PARTS // LOADS
    for n in range(LOADS):
        for kind in range(2):
            loads[n][kind].wait()
        for kind in range(2):
            for part in range(n * run, (n + 1) * run):
                rows = slice(part * depth, (part + 1) * depth)
                turned = pltpu.roll(blocks[kind, rows, :], lax.rem((NZ - z) * piece, width), 1).T
                slices[mine, part, kind] = turned[0:piece]
        if n == 0:
            pl.semaphore_wait(barrier, jnp.where(home, 14, 18) - len(DOUBLE))

        @pl.when(home)
        def _():
            for part in range(n * run, (n + 1) * run):
                spread(part)

        @pl.when(away)
        def _():
            for part in range(n * run, (n + 1) * run):
                cross(part).start()

        for kind in range(2):
            rows = slice(n * run * depth, (n + 1) * run * depth)
            hi, lo = split(blocks[kind, rows, :])
            rhs[kind, rows, 0:width] = hi
            rhs[kind, rows, width:] = lo

    for copy in small:
        copy.wait()
    rows = lax.broadcasted_iota(jnp.int32, (16, 1), 0)
    moments = jnp.zeros((16, 1), F32)
    for row in range(16):
        moment = time_ref[pair_ref[2 * (row % 8) + row // 8]]
        moments = jnp.where(rows == row, moment, moments)
    weights[0] = jnp.exp(-energies[0] * moments)
    weights[1] = jnp.exp(energies[1] * moments)

    @pl.when(away)
    def _():
        for part in range(PARTS):
            cross(part).wait_recv()
            spread(part)

    def slot_of(q):
        return (block_of(q) < blk).astype(jnp.int32)

    def compute(work):
        rows = 128 * len(work)
        tiles = []
        for kind in range(2):
            for n, (q, at, u) in enumerate(work):
                for part in range(PARTS):
                    columns = slice(part * depth, (part + 1) * depth)
                    values = slices[q, part, kind]
                    factors = weights[kind, pl.ds(pl.multiple_of(u * 8, 8), 8), columns]
                    for p in range(8):
                        hi, lo = split(values * factors[p:p + 1, :])
                        lhs[kind, n * 128 + p * piece:n * 128 + (p + 1) * piece, columns] = hi
                        lhs[kind, rows + n * 128 + p * piece:rows + n * 128 + (p + 1) * piece, columns] = lo
            total = jnp.dot(lhs[kind, 0:2 * rows], rhs[kind], preferred_element_type=F32)
            tiles.append((total[0:rows, 0:width]
                          + (total[0:rows, width:] + (total[rows:, 0:width] + total[rows:, width:]))))
        product = -(tiles[0] * tiles[1])
        for n, (q, at, u) in enumerate(work):
            outgoing[at] = product[n * 128:(n + 1) * 128].reshape(NZ, piece, width)
            arrived[at, pl.ds(pl.multiple_of(z * piece, piece), piece), :] = outgoing[at, z]

    def rows_of(plane):
        return pl.ds(pl.multiple_of(plane * piece, piece), piece)

    def far_first(n):
        return 4 + lax.div(n + 1, 2) * (1 - 2 * lax.rem(n, 2))

    def z_copy(first, count, step):
        to = lax.rem(z + step, NZ)
        these = pl.ds(first, count)
        return pltpu.make_async_remote_copy(
            src_ref=outgoing.at[these, to], dst_ref=arrived.at[these, rows_of(z)],
            send_sem=z_send.at[first], recv_sem=z_recv.at[first, step], device_id=z_peer(step), device_id_type=MESH)

    def share(first, count):
        @pl.loop(0, NZ - 1)
        def _(n):
            z_copy(first, count, far_first(n)).start()

    def columns_of(k):
        return pl.ds(pl.multiple_of(k * width, width), width)

    def mirror_copy(q, plane):
        return pltpu.make_async_remote_copy(
            src_ref=arrived.at[q, rows_of(plane)], dst_ref=out_ref.at[0, slot_of(q), rows_of(plane), columns_of(column)],
            send_sem=mirror_send.at[q], recv_sem=mirror_recv.at[column], device_id=mirror_of(q), device_id_type=MESH)

    def mirror(q, plane):
        if q in DOUBLE:
            return
        if q == 0:
            pl.when(away)(mirror_copy(q, plane).start)
        else:
            mirror_copy(q, plane).start()

    def gathered(q):
        whole = slices.at[q]
        pltpu.make_async_copy(whole, whole, ag_recv.at[q, 0]).wait()

    def relay(part):
        gather_copy(slices.at[0], 2, part, down, 2).wait_recv()
        gather_copy(slices.at[2], 4, part, sibling, 4).start()
        gather_copy(slices.at[0], 3, part, up, 1).wait_recv()
        gather_copy(slices.at[3], 5, part, sibling, 5).start()

        @pl.when(c == 1)
        def _():
            gather_copy(slices.at[2], 6, part, down, 6).start()

        @pl.when(c == 0)
        def _():
            gather_copy(slices.at[3], 6, part, up, 6).start()

    def relay_far(part):
        gather_copy(slices.at[3], 6, part, up, 6).wait_recv()
        gather_copy(slices.at[6], 7, part, sibling, 7).start()

    def receive(first, count):
        @pl.loop(0, NZ - 1)
        def _(n):
            step = far_first(n)
            plane = lax.rem(z + NZ - step, NZ)
            here = arrived.at[pl.ds(first, count), rows_of(plane)]
            pltpu.make_async_copy(here, here, z_recv.at[first, step]).wait()
            for q in range(first, first + count):
                if q < 8:
                    mirror(q, plane)

    def place(q, at, u):
        out_ref[0, u, :, columns_of(lax.rem(block_of(q), 8))] = arrived[at].T

    def work(at):
        q = at if at < 8 else (0, 7, 6)[at - 8]
        u = slot_of(q)
        return (q, at, u if at < 8 else 1 - u)

    def make(first, count):
        compute([work(at) for at in range(first, first + count)])
        share(first, count)
        for q in range(first, first + count):
            if q < 8:
                mirror(q, z)

    def finish(first, count):
        receive(first, count)
        for at in range(first, first + count):
            place(*work(at))

    def each(action, parts):
        for part in parts:
            action(part)

    early, late = range(PARTS // 2), range(PARTS // 2, PARTS)

    @pl.when(home)
    def _():
        compute([work(0), work(8)])
        share(0, 1)
        share(8, 1)

    each(relay, early)

    @pl.when(away)
    def _():
        make(0, 1)

    gathered(1)
    make(1, 1)
    each(relay, late)
    make(2, 2)
    each(relay_far, early)
    gathered(4)
    gathered(5)
    make(4, 2)
    finish(0, 1)
    finish(1, 1)

    @pl.when(home)
    def _():
        finish(8, 1)

    each(relay_far, late)
    make(6, 1)
    if 6 in DOUBLE:
        make(10, 1)
    gathered(7)
    make(7, 1)
    if 7 in DOUBLE:
        make(9, 1)
    finish(2, 2)
    finish(4, 2)
    finish(6, 1)
    if 6 in DOUBLE:
        finish(10, 1)
    finish(7, 1)
    if 7 in DOUBLE:
        finish(9, 1)

    for q in range(8):
        if q in DOUBLE:
            continue

        def mirror_arrival(q=q):
            into = out_ref.at[0, 0, :, columns_of(0)]
            pltpu.make_async_copy(into, into, mirror_recv.at[lax.rem(block_of(q), 8)]).wait()
            whole = arrived.at[q]
            pltpu.make_async_copy(whole, whole, mirror_send.at[q]).wait()

        if q == 0:
            pl.when(away)(mirror_arrival)
        else:
            mirror_arrival()

    def sent(first, count):
        rest = outgoing.at[pl.ds(first, count), pl.ds(0, NZ - 1)]
        pltpu.make_async_copy(rest, rest, z_send.at[first]).wait()

    for n in range(1, 8):
        whole = slices.at[0]
        pltpu.make_async_copy(whole, whole, ag_send.at[n]).wait()

    for first, count in ((0, 1), (1, 1), (2, 2), (4, 2), (6, 1), (7, 1)):
        sent(first, count)
    for q in DOUBLE:
        sent({7: 9, 6: 10}[q], 1)

    @pl.when(home)
    def _():
        sent(8, 1)

    @pl.when(away)
    def _():
        pltpu.make_async_copy(own, own, ag_send.at[0]).wait()


def body(occupied_orbitals, empty_orbitals, occupied_energy, empty_energy, time_points, pair_table):
    states, width = occupied_orbitals.shape
    piece = width // NZ
    depth = states // PARTS
    return pl.pallas_call(
        kernel,
        out_shape=pltpu.VMEM((1, 2, width, 8 * width), F32),
        in_specs=[pl.BlockSpec(memory_space=pltpu.HBM)] * 6,
        out_specs=pl.BlockSpec(memory_space=pltpu.VMEM),
        scratch_shapes=[
            pltpu.VMEM((2, states, width), F32),
            pltpu.VMEM((2, 1, states), F32),
            pltpu.SMEM((16,), F32),
            pltpu.SMEM((16,), jnp.int32),
            pltpu.VMEM((9, PARTS, 2, piece, depth), F32),
            pltpu.VMEM((2, states, 2 * width), BF16),
            pltpu.VMEM((2, 512, states), BF16),
            pltpu.VMEM((2, 16, states), F32),
            pltpu.VMEM((11, NZ, piece, width), F32),
            pltpu.VMEM((11, width, width), F32),
            pltpu.SemaphoreType.DMA((LOADS, 2)),
            pltpu.SemaphoreType.DMA((4,)),
            pltpu.SemaphoreType.DMA((8,)),
            pltpu.SemaphoreType.DMA((8, PARTS)),
            pltpu.SemaphoreType.DMA((11,)),
            pltpu.SemaphoreType.DMA((11, NZ)),
            pltpu.SemaphoreType.DMA((8,)),
            pltpu.SemaphoreType.DMA((8,)),
        ],
        compiler_params=pltpu.CompilerParams(
            collective_id=0, has_side_effects=True, vmem_limit_bytes=61 * 2**20),
        cost_estimate=pl.CostEstimate(flops=2**33, bytes_accessed=2**22, transcendentals=2**16),
        name="polarizability",
    )(occupied_orbitals, empty_orbitals, occupied_energy.reshape(1, states), empty_energy.reshape(1, states),
      time_points, pair_table)


def solution(mesh):
    return jax.shard_map(
        body,
        mesh=mesh,
        in_specs=(P(None, "blk"), P(None, "blk"), P(), P(), P(), P()),
        out_specs=P("tm", None, "blk", None),
        check_vma=False,
    )
```

```python
import jax
import jax.numpy as jnp
from jax import lax
from jax.experimental import pallas as pl
from jax.experimental.pallas import tpu as pltpu
from jax.sharding import PartitionSpec as P

MESH = pl.DeviceIdType.MESH
NZ = 8
NY = 4
PARTS = 8
LOADS = 4
SLOTS = ((0, 0), (0, 1), (1, 0), (3, 0), (1, 1), (3, 1), (2, 0), (2, 1))
DIRECT = (0, 2, 3, 6)
DOUBLE = (7, 6)
PLACES = (0, 1, 2, 3, 4, 5, 6, 6, 7, 7, 0)
F32 = jnp.float32
BF16 = jnp.bfloat16


def split(value):
    hi = value.astype(BF16)
    lo = (value - hi.astype(F32)).astype(BF16)
    return hi, lo


def kernel(occ_hbm, emp_hbm, occ_e_hbm, emp_e_hbm, time_hbm, pair_hbm, out_ref,
           blocks, energies, time_ref, pair_ref, slices, rhs, lhs, weights, outgoing, arrived,
           load_sem, small_sem, ag_send, ag_recv, z_send, z_recv, mirror_send, mirror_recv):
    states, width = blocks.shape[1:]
    piece = width // NZ
    depth = states // PARTS
    own = slices.at[8]
    blk, tm = lax.axis_index("blk"), lax.axis_index("tm")
    x_hi, y, c = lax.div(blk, 8), lax.rem(lax.div(blk, 2), NY), lax.rem(blk, 2)
    z, half = lax.div(tm, 2), lax.rem(tm, 2)
    home = x_hi == half
    away = jnp.logical_not(home)
    column = lax.rem(blk, 8)

    def in_column(y_to, c_to):
        return (x_hi * 8 + lax.rem(y_to, NY) * 2 + c_to, tm)

    sibling = in_column(y, 1 - c)
    up, down = in_column(y + 1, c), in_column(y + 3, c)
    across = (half * 8 + y * 2 + c, z * 2 + x_hi)

    def z_peer(step):
        return (blk, lax.rem(z + step, NZ) * 2 + half)

    def block_of(q):
        dy, flip = SLOTS[q]
        return half * 8 + lax.rem(y + dy, NY) * 2 + lax.rem(c + flip, 2)

    def mirror_of(q):
        return (block_of(q), z * 2 + x_hi)

    loads = []
    for n in range(LOADS):
        rows = pl.ds(n * (states // LOADS), states // LOADS)
        loads.append([pltpu.make_async_copy(ref.at[rows], blocks.at[kind, rows], load_sem.at[n, kind])
                      for kind, ref in enumerate((emp_hbm, occ_hbm))])
    small = [pltpu.make_async_copy(source, to, small_sem.at[n]) for n, (source, to) in enumerate((
        (emp_e_hbm, energies.at[0]), (occ_e_hbm, energies.at[1]), (time_hbm, time_ref), (pair_hbm, pair_ref)))]
    for copy in loads[0]:
        copy.start()

    barrier = pltpu.get_barrier_semaphore()

    def greet(device):
        pl.semaphore_signal(barrier, inc=1, device_id=device, device_id_type=MESH)

    @pl.loop(1, NZ)
    def _(step):
        greet(z_peer(step))

    for q in range(1, 8):
        if q not in DOUBLE:
            greet(mirror_of(q))

    @pl.when(away)
    def _():
        greet(across)
        greet(sibling)
        greet(up)
        greet(down)

    for pair in loads[1:]:
        for copy in pair:
            copy.start()
    for copy in small:
        copy.start()

    def gather_copy(source, at, part, device, n):
        return pltpu.make_async_remote_copy(
            src_ref=source.at[part], dst_ref=slices.at[at, part], send_sem=ag_send.at[n],
            recv_sem=ag_recv.at[at, part if at in DIRECT else 0], device_id=device, device_id_type=MESH)

    def cross(part):
        return gather_copy(own, 0, part, across, 0)

    def spread(part):
        for at, device, n in ((3, up, 1), (2, down, 2), (1, sibling, 3)):
            gather_copy(slices.at[0], at, part, device, n).start()

    mine = jnp.where(home, 0, 8)
    run = PARTS // LOADS
    for n in range(LOADS):
        for kind in range(2):
            loads[n][kind].wait()
        for kind in range(2):
            for part in range(n * run, (n + 1) * run):
                rows = slice(part * depth, (part + 1) * depth)
                turned = pltpu.roll(blocks[kind, rows, :], lax.rem((NZ - z) * piece, width), 1).T
                slices[mine, part, kind] = turned[0:piece]
        if n == 0:
            pl.semaphore_wait(barrier, jnp.where(home, 14, 18) - len(DOUBLE))

        @pl.when(home)
        def _():
            for part in range(n * run, (n + 1) * run):
                spread(part)

        @pl.when(away)
        def _():
            for part in range(n * run, (n + 1) * run):
                cross(part).start()

        for kind in range(2):
            rows = slice(n * run * depth, (n + 1) * run * depth)
            hi, lo = split(blocks[kind, rows, :])
            rhs[kind, rows, 0:width] = hi
            rhs[kind, rows, width:] = lo

    for copy in small:
        copy.wait()
    rows = lax.broadcasted_iota(jnp.int32, (16, 1), 0)
    moments = jnp.zeros((16, 1), F32)
    for row in range(16):
        moment = time_ref[pair_ref[2 * (row % 8) + row // 8]]
        moments = jnp.where(rows == row, moment, moments)
    weights[0] = jnp.exp(-energies[0] * moments)
    weights[1] = jnp.exp(energies[1] * moments)

    @pl.when(away)
    def _():
        for part in range(PARTS):
            cross(part).wait_recv()
            spread(part)

    def slot_of(q):
        return (block_of(q) < blk).astype(jnp.int32)

    def compute(work):
        rows = 128 * len(work)
        tiles = []
        for kind in range(2):
            for n, (q, at, u) in enumerate(work):
                for part in range(PARTS):
                    columns = slice(part * depth, (part + 1) * depth)
                    values = slices[q, part, kind]
                    factors = weights[kind, pl.ds(pl.multiple_of(u * 8, 8), 8), columns]
                    for p in range(8):
                        hi, lo = split(values * factors[p:p + 1, :])
                        lhs[kind, n * 128 + p * piece:n * 128 + (p + 1) * piece, columns] = hi
                        lhs[kind, rows + n * 128 + p * piece:rows + n * 128 + (p + 1) * piece, columns] = lo
            total = jnp.dot(lhs[kind, 0:2 * rows], rhs[kind], preferred_element_type=F32)
            tiles.append((total[0:rows, 0:width]
                          + (total[0:rows, width:] + (total[rows:, 0:width] + total[rows:, width:]))))
        product = -(tiles[0] * tiles[1])
        for n, (q, at, u) in enumerate(work):
            outgoing[at] = product[n * 128:(n + 1) * 128].reshape(NZ, piece, width)
            arrived[at, pl.ds(pl.multiple_of(z * piece, piece), piece), :] = outgoing[at, z]

    def rows_of(plane):
        return pl.ds(pl.multiple_of(plane * piece, piece), piece)

    def far_first(n):
        return 4 + lax.div(n + 1, 2) * (1 - 2 * lax.rem(n, 2))

    def z_copy(first, count, step):
        to = lax.rem(z + step, NZ)
        these = pl.ds(first, count)
        return pltpu.make_async_remote_copy(
            src_ref=outgoing.at[these, to], dst_ref=arrived.at[these, rows_of(z)],
            send_sem=z_send.at[first], recv_sem=z_recv.at[first, step], device_id=z_peer(step), device_id_type=MESH)

    def share(first, count):
        @pl.loop(0, NZ - 1)
        def _(n):
            z_copy(first, count, far_first(n)).start()

    def columns_of(k):
        return pl.ds(pl.multiple_of(k * width, width), width)

    def mirror_copy(q, plane):
        return pltpu.make_async_remote_copy(
            src_ref=arrived.at[q, rows_of(plane)], dst_ref=out_ref.at[0, slot_of(q), rows_of(plane), columns_of(column)],
            send_sem=mirror_send.at[q], recv_sem=mirror_recv.at[column], device_id=mirror_of(q), device_id_type=MESH)

    def mirror(q, plane):
        if q in DOUBLE:
            return
        if q == 0:
            pl.when(away)(mirror_copy(q, plane).start)
        else:
            mirror_copy(q, plane).start()

    def gathered(q):
        whole = slices.at[q]
        pltpu.make_async_copy(whole, whole, ag_recv.at[q, 0]).wait()

    def relay(part):
        gather_copy(slices.at[0], 2, part, down, 2).wait_recv()
        gather_copy(slices.at[2], 4, part, sibling, 4).start()
        gather_copy(slices.at[0], 3, part, up, 1).wait_recv()
        gather_copy(slices.at[3], 5, part, sibling, 5).start()

        @pl.when(c == 1)
        def _():
            gather_copy(slices.at[2], 6, part, down, 6).start()

        @pl.when(c == 0)
        def _():
            gather_copy(slices.at[3], 6, part, up, 6).start()

    def relay_far(part):
        gather_copy(slices.at[3], 6, part, up, 6).wait_recv()
        gather_copy(slices.at[6], 7, part, sibling, 7).start()

    def receive(first, count):
        @pl.loop(0, NZ - 1)
        def _(n):
            step = far_first(n)
            plane = lax.rem(z + NZ - step, NZ)
            here = arrived.at[pl.ds(first, count), rows_of(plane)]
            pltpu.make_async_copy(here, here, z_recv.at[first, step]).wait()
            for q in range(first, first + count):
                if q < 6:
                    mirror(q, plane)

    def place(q, at, u):
        out_ref[0, u, :, columns_of(lax.rem(block_of(q), 8))] = arrived[at].T

    def work(at):
        q = PLACES[at]
        u = slot_of(q)
        return (q, at, 1 - u if at in (7, 9, 10) else u)

    def make(first, count):
        compute([work(at) for at in range(first, first + count)])
        share(first, count)
        for q in range(first, first + count):
            if q < 6:
                mirror(q, z)

    def finish(first, count):
        receive(first, count)
        for at in range(first, first + count):
            place(*work(at))

    def each(action, parts):
        for part in parts:
            action(part)

    early, late = range(PARTS // 2), range(PARTS // 2, PARTS)

    @pl.when(home)
    def _():
        compute([work(0), work(10)])
        share(0, 1)
        share(10, 1)

    @pl.when(away)
    def _():
        make(0, 1)

    @pl.when(home)
    def _():
        gathered(1)
        make(1, 1)

    each(relay, early)

    @pl.when(away)
    def _():
        gathered(1)
        make(1, 1)

    each(relay, late)
    make(2, 2)
    each(relay_far, early)
    gathered(4)
    gathered(5)
    make(4, 2)
    each(relay_far, late)
    make(6, 2)
    finish(0, 1)
    finish(1, 1)

    @pl.when(home)
    def _():
        finish(10, 1)

    gathered(7)
    make(8, 2)
    finish(2, 2)
    finish(4, 2)
    finish(6, 2)
    finish(8, 2)

    for q in range(8):
        if q in DOUBLE:
            continue

        def mirror_arrival(q=q):
            into = out_ref.at[0, 0, :, columns_of(0)]
            pltpu.make_async_copy(into, into, mirror_recv.at[lax.rem(block_of(q), 8)]).wait()
            whole = arrived.at[q]
            pltpu.make_async_copy(whole, whole, mirror_send.at[q]).wait()

        if q == 0:
            pl.when(away)(mirror_arrival)
        else:
            mirror_arrival()

    def sent(first, count):
        rest = outgoing.at[pl.ds(first, count), pl.ds(0, NZ - 1)]
        pltpu.make_async_copy(rest, rest, z_send.at[first]).wait()

    for n in range(1, 8):
        whole = slices.at[0]
        pltpu.make_async_copy(whole, whole, ag_send.at[n]).wait()

    for first, count in ((0, 1), (1, 1), (2, 2), (4, 2), (6, 2), (8, 2)):
        sent(first, count)

    @pl.when(home)
    def _():
        sent(10, 1)

    @pl.when(away)
    def _():
        pltpu.make_async_copy(own, own, ag_send.at[0]).wait()


def body(occupied_orbitals, empty_orbitals, occupied_energy, empty_energy, time_points, pair_table):
    states, width = occupied_orbitals.shape
    piece = width // NZ
    depth = states // PARTS
    return pl.pallas_call(
        kernel,
        out_shape=pltpu.VMEM((1, 2, width, 8 * width), F32),
        in_specs=[pl.BlockSpec(memory_space=pltpu.HBM)] * 6,
        out_specs=pl.BlockSpec(memory_space=pltpu.VMEM),
        scratch_shapes=[
            pltpu.VMEM((2, states, width), F32),
            pltpu.VMEM((2, 1, states), F32),
            pltpu.SMEM((16,), F32),
            pltpu.SMEM((16,), jnp.int32),
            pltpu.VMEM((9, PARTS, 2, piece, depth), F32),
            pltpu.VMEM((2, states, 2 * width), BF16),
            pltpu.VMEM((2, 512, states), BF16),
            pltpu.VMEM((2, 16, states), F32),
            pltpu.VMEM((11, NZ, piece, width), F32),
            pltpu.VMEM((11, width, width), F32),
            pltpu.SemaphoreType.DMA((LOADS, 2)),
            pltpu.SemaphoreType.DMA((4,)),
            pltpu.SemaphoreType.DMA((8,)),
            pltpu.SemaphoreType.DMA((8, PARTS)),
            pltpu.SemaphoreType.DMA((11,)),
            pltpu.SemaphoreType.DMA((11, NZ)),
            pltpu.SemaphoreType.DMA((8,)),
            pltpu.SemaphoreType.DMA((8,)),
        ],
        compiler_params=pltpu.CompilerParams(
            collective_id=0, has_side_effects=True, vmem_limit_bytes=61 * 2**20),
        cost_estimate=pl.CostEstimate(flops=2**33, bytes_accessed=2**22, transcendentals=2**16),
        name="polarizability",
    )(occupied_orbitals, empty_orbitals, occupied_energy.reshape(1, states), empty_energy.reshape(1, states),
      time_points, pair_table)


def solution(mesh):
    return jax.shard_map(
        body,
        mesh=mesh,
        in_specs=(P(None, "blk"), P(None, "blk"), P(), P(), P(), P()),
        out_specs=P("tm", None, "blk", None),
        check_vma=False,
    )
```

```python
import jax
import jax.numpy as jnp
from jax import lax
from jax.experimental import pallas as pl
from jax.experimental.pallas import tpu as pltpu
from jax.sharding import PartitionSpec as P

MESH = pl.DeviceIdType.MESH
NZ = 8
NY = 4
PARTS = 8
LOADS = 4
SLOTS = ((0, 0), (0, 1), (1, 0), (3, 0), (1, 1), (3, 1), (2, 0), (2, 1))
DIRECT = (0, 2, 3, 6)
DOUBLE = (7, 6)
PLACES = (0, 1, 2, 3, 4, 5, 6, 6, 7, 7, 0)
F32 = jnp.float32
BF16 = jnp.bfloat16


def split(value):
    hi = value.astype(BF16)
    lo = (value - hi.astype(F32)).astype(BF16)
    return hi, lo


def kernel(occ_hbm, emp_hbm, occ_e_hbm, emp_e_hbm, time_hbm, pair_hbm, out_ref,
           blocks, energies, time_ref, pair_ref, slices, rhs, lhs, weights, outgoing, arrived,
           load_sem, small_sem, ag_send, ag_recv, z_send, z_recv, mirror_send, mirror_recv):
    states, width = blocks.shape[1:]
    piece = width // NZ
    depth = states // PARTS
    own = slices.at[8]
    blk, tm = lax.axis_index("blk"), lax.axis_index("tm")
    x_hi, y, c = lax.div(blk, 8), lax.rem(lax.div(blk, 2), NY), lax.rem(blk, 2)
    z, half = lax.div(tm, 2), lax.rem(tm, 2)
    home = x_hi == half
    away = jnp.logical_not(home)
    column = lax.rem(blk, 8)

    def in_column(y_to, c_to):
        return (x_hi * 8 + lax.rem(y_to, NY) * 2 + c_to, tm)

    sibling = in_column(y, 1 - c)
    up, down = in_column(y + 1, c), in_column(y + 3, c)
    across = (half * 8 + y * 2 + c, z * 2 + x_hi)

    def z_peer(step):
        return (blk, lax.rem(z + step, NZ) * 2 + half)

    def block_of(q):
        dy, flip = SLOTS[q]
        return half * 8 + lax.rem(y + dy, NY) * 2 + lax.rem(c + flip, 2)

    def mirror_of(q):
        return (block_of(q), z * 2 + x_hi)

    loads = []
    for n in range(LOADS):
        rows = pl.ds(n * (states // LOADS), states // LOADS)
        loads.append([pltpu.make_async_copy(ref.at[rows], blocks.at[kind, rows], load_sem.at[n, kind])
                      for kind, ref in enumerate((emp_hbm, occ_hbm))])
    small = [pltpu.make_async_copy(source, to, small_sem.at[n]) for n, (source, to) in enumerate((
        (emp_e_hbm, energies.at[0]), (occ_e_hbm, energies.at[1]), (time_hbm, time_ref), (pair_hbm, pair_ref)))]
    for copy in loads[0]:
        copy.start()

    barrier = pltpu.get_barrier_semaphore()

    def greet(device):
        pl.semaphore_signal(barrier, inc=1, device_id=device, device_id_type=MESH)

    @pl.loop(1, NZ)
    def _(step):
        greet(z_peer(step))

    for q in range(1, 8):
        if q not in DOUBLE:
            greet(mirror_of(q))

    @pl.when(away)
    def _():
        greet(across)
        greet(sibling)
        greet(up)
        greet(down)

    for pair in loads[1:]:
        for copy in pair:
            copy.start()
    for copy in small:
        copy.start()

    def gather_copy(source, at, part, device, n):
        return pltpu.make_async_remote_copy(
            src_ref=source.at[part], dst_ref=slices.at[at, part], send_sem=ag_send.at[n],
            recv_sem=ag_recv.at[at, part if at in DIRECT else 0], device_id=device, device_id_type=MESH)

    def cross(part):
        return gather_copy(own, 0, part, across, 0)

    def spread(part):
        for at, device, n in ((3, up, 1), (2, down, 2), (1, sibling, 3)):
            gather_copy(slices.at[0], at, part, device, n).start()

    mine = jnp.where(home, 0, 8)
    run = PARTS // LOADS
    for n in range(LOADS):
        for kind in range(2):
            loads[n][kind].wait()
        for kind in range(2):
            for part in range(n * run, (n + 1) * run):
                rows = slice(part * depth, (part + 1) * depth)
                turned = pltpu.roll(blocks[kind, rows, :], lax.rem((NZ - z) * piece, width), 1).T
                slices[mine, part, kind] = turned[0:piece]
        if n == 0:
            pl.semaphore_wait(barrier, jnp.where(home, 14, 18) - len(DOUBLE))

        @pl.when(home)
        def _():
            for part in range(n * run, (n + 1) * run):
                spread(part)

        @pl.when(away)
        def _():
            for part in range(n * run, (n + 1) * run):
                cross(part).start()

        for kind in range(2):
            rows = slice(n * run * depth, (n + 1) * run * depth)
            hi, lo = split(blocks[kind, rows, :])
            rhs[kind, rows, 0:width] = hi
            rhs[kind, rows, width:] = lo

    for copy in small:
        copy.wait()
    rows = lax.broadcasted_iota(jnp.int32, (16, 1), 0)
    moments = jnp.zeros((16, 1), F32)
    for row in range(16):
        moment = time_ref[pair_ref[2 * (row % 8) + row // 8]]
        moments = jnp.where(rows == row, moment, moments)
    weights[0] = jnp.exp(-energies[0] * moments)
    weights[1] = jnp.exp(energies[1] * moments)

    @pl.when(away)
    def _():
        for part in range(PARTS):
            cross(part).wait_recv()
            spread(part)

    def slot_of(q):
        return (block_of(q) < blk).astype(jnp.int32)

    def compute(work):
        rows = 128 * len(work)
        tiles = []
        for kind in range(2):
            for n, (q, at, u) in enumerate(work):
                for part in range(PARTS):
                    columns = slice(part * depth, (part + 1) * depth)
                    values = slices[q, part, kind]
                    factors = weights[kind, pl.ds(pl.multiple_of(u * 8, 8), 8), columns]
                    for p in range(8):
                        hi, lo = split(values * factors[p:p + 1, :])
                        lhs[kind, n * 128 + p * piece:n * 128 + (p + 1) * piece, columns] = hi
                        lhs[kind, rows + n * 128 + p * piece:rows + n * 128 + (p + 1) * piece, columns] = lo
            total = jnp.dot(lhs[kind, 0:2 * rows], rhs[kind], preferred_element_type=F32)
            tiles.append((total[0:rows, 0:width]
                          + (total[0:rows, width:] + (total[rows:, 0:width] + total[rows:, width:]))))
        product = -(tiles[0] * tiles[1])
        for n, (q, at, u) in enumerate(work):
            outgoing[at] = product[n * 128:(n + 1) * 128].reshape(NZ, piece, width)
            arrived[at, pl.ds(pl.multiple_of(z * piece, piece), piece), :] = outgoing[at, z]

    def rows_of(plane):
        return pl.ds(pl.multiple_of(plane * piece, piece), piece)

    def far_first(n):
        return 4 + lax.div(n + 1, 2) * (1 - 2 * lax.rem(n, 2))

    def z_copy(first, count, step):
        to = lax.rem(z + step, NZ)
        these = pl.ds(first, count)
        return pltpu.make_async_remote_copy(
            src_ref=outgoing.at[these, to], dst_ref=arrived.at[these, rows_of(z)],
            send_sem=z_send.at[first], recv_sem=z_recv.at[first, step], device_id=z_peer(step), device_id_type=MESH)

    def share(first, count):
        for step in (4, 3, 5, 2, 6, 1, 7):
            z_copy(first, count, step).start()

    def columns_of(k):
        return pl.ds(pl.multiple_of(k * width, width), width)

    def mirror_copy(q, plane):
        return pltpu.make_async_remote_copy(
            src_ref=arrived.at[q, rows_of(plane)], dst_ref=out_ref.at[0, slot_of(q), rows_of(plane), columns_of(column)],
            send_sem=mirror_send.at[q], recv_sem=mirror_recv.at[column], device_id=mirror_of(q), device_id_type=MESH)

    def mirror(q, plane):
        if q in DOUBLE:
            return
        if q == 0:
            pl.when(away)(mirror_copy(q, plane).start)
        else:
            mirror_copy(q, plane).start()

    def gathered(q):
        whole = slices.at[q]
        pltpu.make_async_copy(whole, whole, ag_recv.at[q, 0]).wait()

    def relay(part):
        gather_copy(slices.at[0], 2, part, down, 2).wait_recv()
        gather_copy(slices.at[2], 4, part, sibling, 4).start()
        gather_copy(slices.at[0], 3, part, up, 1).wait_recv()
        gather_copy(slices.at[3], 5, part, sibling, 5).start()

        @pl.when(c == 1)
        def _():
            gather_copy(slices.at[2], 6, part, down, 6).start()

        @pl.when(c == 0)
        def _():
            gather_copy(slices.at[3], 6, part, up, 6).start()

    def relay_far(part):
        gather_copy(slices.at[3], 6, part, up, 6).wait_recv()
        gather_copy(slices.at[6], 7, part, sibling, 7).start()

    def receive(first, count):
        @pl.loop(0, NZ - 1)
        def _(n):
            step = far_first(n)
            plane = lax.rem(z + NZ - step, NZ)
            here = arrived.at[pl.ds(first, count), rows_of(plane)]
            pltpu.make_async_copy(here, here, z_recv.at[first, step]).wait()
            for q in range(first, first + count):
                if q < 6:
                    mirror(q, plane)

    def place(q, at, u):
        out_ref[0, u, :, columns_of(lax.rem(block_of(q), 8))] = arrived[at].T

    def work(at):
        q = PLACES[at]
        u = slot_of(q)
        return (q, at, 1 - u if at in (7, 9, 10) else u)

    def make(first, count):
        compute([work(at) for at in range(first, first + count)])
        share(first, count)
        for q in range(first, first + count):
            if q < 6:
                mirror(q, z)

    def finish(first, count):
        receive(first, count)
        for at in range(first, first + count):
            place(*work(at))

    def each(action, parts):
        for part in parts:
            action(part)

    early, late = range(PARTS // 2), range(PARTS // 2, PARTS)

    @pl.when(home)
    def _():
        compute([work(0), work(10)])
        share(0, 1)
        share(10, 1)

    @pl.when(away)
    def _():
        make(0, 1)

    @pl.when(home)
    def _():
        gathered(1)
        make(1, 1)

    each(relay, early)

    @pl.when(away)
    def _():
        gathered(1)
        make(1, 1)

    each(relay, late)
    make(2, 2)
    each(relay_far, early)
    gathered(4)
    gathered(5)
    make(4, 2)
    each(relay_far, late)
    make(6, 2)
    finish(0, 1)
    finish(1, 1)

    @pl.when(home)
    def _():
        finish(10, 1)

    gathered(7)
    finish(2, 2)
    make(8, 2)
    finish(4, 2)
    finish(6, 2)
    finish(8, 2)

    for q in range(8):
        if q in DOUBLE:
            continue

        def mirror_arrival(q=q):
            into = out_ref.at[0, 0, :, columns_of(0)]
            pltpu.make_async_copy(into, into, mirror_recv.at[lax.rem(block_of(q), 8)]).wait()
            whole = arrived.at[q]
            pltpu.make_async_copy(whole, whole, mirror_send.at[q]).wait()

        if q == 0:
            pl.when(away)(mirror_arrival)
        else:
            mirror_arrival()

    def sent(first, count):
        rest = outgoing.at[pl.ds(first, count), pl.ds(0, NZ - 1)]
        pltpu.make_async_copy(rest, rest, z_send.at[first]).wait()

    for n in range(1, 8):
        whole = slices.at[0]
        pltpu.make_async_copy(whole, whole, ag_send.at[n]).wait()

    for first, count in ((0, 1), (1, 1), (2, 2), (4, 2), (6, 2), (8, 2)):
        sent(first, count)

    @pl.when(home)
    def _():
        sent(10, 1)

    @pl.when(away)
    def _():
        pltpu.make_async_copy(own, own, ag_send.at[0]).wait()


def body(occupied_orbitals, empty_orbitals, occupied_energy, empty_energy, time_points, pair_table):
    states, width = occupied_orbitals.shape
    piece = width // NZ
    depth = states // PARTS
    return pl.pallas_call(
        kernel,
        out_shape=pltpu.VMEM((1, 2, width, 8 * width), F32),
        in_specs=[pl.BlockSpec(memory_space=pltpu.HBM)] * 6,
        out_specs=pl.BlockSpec(memory_space=pltpu.VMEM),
        scratch_shapes=[
            pltpu.VMEM((2, states, width), F32),
            pltpu.VMEM((2, 1, states), F32),
            pltpu.SMEM((16,), F32),
            pltpu.SMEM((16,), jnp.int32),
            pltpu.VMEM((9, PARTS, 2, piece, depth), F32),
            pltpu.VMEM((2, states, 2 * width), BF16),
            pltpu.VMEM((2, 512, states), BF16),
            pltpu.VMEM((2, 16, states), F32),
            pltpu.VMEM((11, NZ, piece, width), F32),
            pltpu.VMEM((11, width, width), F32),
            pltpu.SemaphoreType.DMA((LOADS, 2)),
            pltpu.SemaphoreType.DMA((4,)),
            pltpu.SemaphoreType.DMA((8,)),
            pltpu.SemaphoreType.DMA((8, PARTS)),
            pltpu.SemaphoreType.DMA((11,)),
            pltpu.SemaphoreType.DMA((11, NZ)),
            pltpu.SemaphoreType.DMA((8,)),
            pltpu.SemaphoreType.DMA((8,)),
        ],
        compiler_params=pltpu.CompilerParams(
            collective_id=0, has_side_effects=True, vmem_limit_bytes=61 * 2**20),
        cost_estimate=pl.CostEstimate(flops=2**33, bytes_accessed=2**22, transcendentals=2**16),
        name="polarizability",
    )(occupied_orbitals, empty_orbitals, occupied_energy.reshape(1, states), empty_energy.reshape(1, states),
      time_points, pair_table)


def solution(mesh):
    return jax.shard_map(
        body,
        mesh=mesh,
        in_specs=(P(None, "blk"), P(None, "blk"), P(), P(), P(), P()),
        out_specs=P("tm", None, "blk", None),
        check_vma=False,
    )
```
